32 devices in a mesh: band: 2 (over x), wide: 8 (over z, y), narrow: 2 (over core).
Axes of the slice: x: 2, y: 2, z: 4, core: 2. Of those that a mesh axis runs over, the one named last changes fastest.
Arguments:
- voltages: bfloat16 [2, 1024, 268288], P(None, ('band', 'narrow', 'wide')), parts along dimension 1, may hold values from -6 to 6
- fir_taps: float32 [4, 2048], replicated, may hold values from -0.046875 to 0.046875
- flags: int32 [1024], P(('band', 'narrow', 'wide')), parts along dimension 0, may hold values 0 or 1
- tile_order: int32 [256], replicated, may hold values from 0 to 255, each once
Outputs:
- visibilities: bfloat16 [128, 2, 512, 512], P(('band', 'wide'), None, 'narrow'), parts along dimension 0
The draws below stay inside these ranges and needn't reach their ends.
There are 2 independent parts, one for each index of `band`. The reference program is written for one: setup_inputs(seed, part) draws one part's arguments, and reference() takes and returns one part's arrays. A program takes and returns all parts, laid end to end along the dimension named above; an argument that names none is the same for every part. Nothing has to cross between parts.
Inputs may be any that keep to these rules, and one draw needn't show every extreme that they name: `tile_order`: each station appears exactly once.
All inputs are finite; a program needn't handle non-finite values. No bound on the sum of `flags` on one device may be relied on, other than what follows from the above.
Results may differ from the reference program's by a relative error of at most 0.0071.
Values may be sent and summed in bfloat16 or wider, within the bound.
A program may use at most 256 MiB of HBM per device.

```python
import math
import jax
import jax.numpy as jnp
from jax import lax

STATIONS = 256
NFFT = 2048
TAPS = 4
TIMES = 128
INPUTS = 512
KEEP = 64
SAMPLES = 268288


def place_ends(array, own_key, low, high):
    longest = array.shape.index(max(array.shape))
    spots = []
    for shift in (0, 1):
        where = [jax.random.randint(jax.random.fold_in(own_key, axis), (), 0, length) for axis, length in enumerate(array.shape)]
        where[longest] = (where[longest] + shift) % array.shape[longest]
        spots.append(tuple(where))
    return array.at[spots[0]].set(low).at[spots[1]].set(high)


def shard_levels(own_key, extent, shards, least, largest):
    def one(axis_at, shards_of):
        steps = jax.random.uniform(jax.random.fold_in(jax.random.fold_in(own_key, 6), axis_at), (shards_of,), jnp.float32, least / len(shards), largest / len(shards))
        return jnp.repeat(jnp.exp(steps), extent[axis_at] // shards_of).reshape((-1,) + (1,) * (len(extent) - axis_at - 1))

    factor_of = one(*shards[0])
    for cut in shards[1:]:
        factor_of = factor_of * one(*cut)
    return factor_of


def noise(own_key, shape, deviation, most, split=(), kind=jnp.bfloat16):
    loudness = shard_levels(own_key, shape, split, -0.22, 0.18) if split else 1.0
    values = jax.random.normal(own_key, shape, jnp.float32) * deviation * loudness
    return jnp.minimum(jnp.maximum(values, -most), most).astype(kind)


def setup_inputs(seed: int = 0, part: int = 0) -> dict:
    key_of = jax.random.split(jax.random.key(seed), 5)
    part_keys = jax.random.split(jax.random.fold_in(key_of[4], part), 5)
    return {
        "voltages": noise(part_keys[0], (2, INPUTS, SAMPLES), 1.0, 6.0, ((1, 16),)),
        "fir_taps": noise(key_of[1], (TAPS, NFFT), (2 * TAPS * NFFT) ** -0.5, 0.046875, (), jnp.float32),
        "flags": place_ends((jax.random.randint(part_keys[2], (INPUTS,), 0, 8) < 7).astype(jnp.int32), jax.random.fold_in(part_keys[2], 1), 0, 1),
        "tile_order": jax.random.permutation(key_of[3], STATIONS).astype(jnp.int32),
    }


def dft_table(points, kept):
    index_n = jnp.arange(points, dtype=jnp.int32)[:, None]
    index_c = jnp.arange(kept, dtype=jnp.int32)[None, :]
    phase = (index_n * index_c) % points
    theta = phase.astype(jnp.float32) * (2.0 * math.pi / points)
    cosine = jnp.cos(theta)
    sine = jnp.sin(theta)
    upper = jnp.stack([cosine, -sine], -1)
    lower = jnp.stack([sine, cosine], -1)
    return jnp.concatenate([upper, lower], 0).astype(jnp.bfloat16)


def filter_bank(block, fir_taps):
    frames = block.astype(jnp.float32).reshape(2, block.shape[1], -1, NFFT)
    steps = frames.shape[2] - TAPS + 1
    total = jnp.zeros((2, block.shape[1], steps, NFFT), jnp.float32)
    for tap in range(TAPS):
        total = total + fir_taps[tap][None, None, None, :] * frames[:, :, tap:tap + steps, :]
    return total.astype(jnp.bfloat16)


def reference(voltages, fir_taps, flags, tile_order):
    table = dft_table(NFFT, KEEP).astype(jnp.float32)
    blocks = voltages.reshape(2, INPUTS // 8, 8, SAMPLES).transpose(1, 0, 2, 3)
    marks = flags.reshape(INPUTS // 8, 8).astype(jnp.float32)

    def channelise(operands):
        block, mark = operands
        filtered = filter_bank(block, fir_taps)
        stacked = jnp.concatenate([filtered[0], filtered[1]], -1).astype(jnp.float32)
        spec = jnp.einsum("itn,ncr->icrt", stacked, table, precision=lax.Precision.HIGHEST)
        spec = spec * mark[:, None, None, None]
        return spec.astype(jnp.bfloat16).reshape(8, KEEP, 2 * TIMES)

    spectra = lax.map(channelise, (blocks, marks)).reshape(INPUTS, KEEP, 2 * TIMES)
    column_index = (2 * tile_order[:, None] + jnp.arange(2, dtype=jnp.int32)[None, :]).reshape(-1)
    columns = jnp.take(spectra, column_index, axis=0)
    rotated = jnp.concatenate([-columns[..., TIMES:], columns[..., :TIMES]], -1)
    paired = jnp.stack([columns, rotated]).astype(jnp.float32)
    rows_all = spectra.astype(jnp.float32)

    def correlate(channel):
        left = rows_all[:, channel, :]
        right = paired[:, :, channel, :]
        tile = jnp.einsum("im,sjm->sij", left, right, precision=lax.Precision.HIGHEST) / TIMES
        return tile.astype(jnp.bfloat16)

    return lax.map(correlate, jnp.arange(KEEP, dtype=jnp.int32))
```

```python
import functools
import math

import jax
import jax.numpy as jnp
import ml_dtypes
import numpy as np
from jax import lax
from jax.experimental import pallas as pl
from jax.experimental.pallas import tpu as pltpu
from jax.sharding import PartitionSpec as P

NFFT = 2048
TAPS = 4
CH_DEV = 8
HALF = 64
MESH = pl.DeviceIdType.MESH


def dft_table(points, kept):
    phase = np.arange(points)[:, None] * np.arange(kept)[None, :] % points
    theta = phase * (2.0 * math.pi / points)
    cosine, sine = np.cos(theta), np.sin(theta)
    upper = np.concatenate([cosine, -sine], 1)
    lower = np.concatenate([sine, cosine], 1)
    return np.concatenate([upper, lower], 0).astype(ml_dtypes.bfloat16)


def channelise(wide, nq, rows, halves, volt, dft, fir, flags, out, frames, table, grid_sum, spec,
               stage, send, in_sem, send_sem, recv_sem, own_sem, fwd_send, fwd_recv):
    me = lax.axis_index("wide")
    core = lax.axis_index("narrow")
    kept = CH_DEV * wide
    span = 2 * kept
    steps = HALF + TAPS - 1
    chunks = nq * halves

    def load(chunk):
        q, th = chunk // halves, chunk % halves

        @pl.loop(0, steps)
        def _(s):
            for part in range(2):
                pltpu.make_async_copy(
                    volt.at[part, pl.ds(q * rows, rows), pl.ds(pl.multiple_of((th * HALF + s) * NFFT, NFFT), NFFT)],
                    frames.at[chunk, s, :, pl.ds(part * NFFT, NFFT)],
                    in_sem.at[chunk],
                ).start()

    for chunk in range(chunks):
        load(chunk)

    barrier = pltpu.get_barrier_semaphore()
    for d in range(1, wide):
        pl.semaphore_signal(barrier, inc=1, device_id={"wide": lax.rem(me + d, wide)}, device_id_type=MESH)
    pl.semaphore_signal(barrier, inc=1, device_id={"narrow": 1 - core}, device_id_type=MESH)

    taps = jnp.concatenate([fir[...], fir[...]], 0).T
    step_n = 256
    for n0 in range(0, NFFT, step_n):
        for part in range(2):
            base = part * NFFT + n0
            w = dft[base : base + step_n, :].astype(jnp.float32)
            for k in range(TAPS):
                table[base : base + step_n, k * span : (k + 1) * span] = (
                    w * taps[n0 : n0 + step_n, k : k + 1]
                ).astype(jnp.bfloat16)

    pl.semaphore_wait(barrier, wide)

    def place(chunk, source):
        q, th = chunk // halves, chunk % halves
        return out.at[th, :, (core * wide + source) * nq + q]

    def to_peer(chunk, peer):
        return pltpu.make_async_remote_copy(
            src_ref=send.at[chunk, pl.ds(peer * CH_DEV, CH_DEV)],
            dst_ref=place(chunk, me),
            send_sem=send_sem,
            recv_sem=recv_sem.at[chunk, me],
            device_id={"wide": peer},
            device_id_type=MESH,
        )

    @pl.loop(0, chunks)
    def _(chunk):
        pltpu.make_async_copy(frames.at[chunk], frames.at[chunk], in_sem.at[chunk]).wait()
        lhs = frames[chunk]
        if rows % 16:
            lhs = lhs.astype(jnp.float32).reshape(steps * rows, 2 * NFFT).astype(jnp.bfloat16)
        else:
            lhs = lhs.reshape(steps * rows, 2 * NFFT)
        grid_sum[...] = jnp.dot(lhs, table[...], preferred_element_type=jnp.float32)
        count = HALF * rows
        total = grid_sum[0:count, 0:span]
        for k in range(1, TAPS):
            total = total + grid_sum[k * rows : k * rows + count, k * span : (k + 1) * span]
        for lane in range(0, span, 128):
            spec[lane // 128] = total[:, lane : lane + 128]
        q = chunk // halves
        for i in range(rows):
            pieces = [spec[b, pl.ds(i, HALF, stride=rows), :] for b in range(span // 128)]
            if kept % 128:
                piece = pieces[0]
                both = jnp.concatenate([piece, pltpu.roll(piece, kept, 1)], 0).T[:kept]
            else:
                mid = kept // 128
                both = jnp.concatenate(
                    [jnp.concatenate([pieces[b], pieces[mid + b]], 0).T for b in range(mid)], 0
                )
            both = both * flags[q * rows + i].astype(jnp.float32)
            stage[pl.ds(i, kept, stride=rows), :] = both
        send[chunk] = stage[...].reshape(kept, rows, 2 * HALF).astype(jnp.bfloat16)
        for d in range(1, wide):
            to_peer(chunk, lax.rem(me + d, wide)).start()
        pltpu.make_async_copy(
            send.at[chunk, pl.ds(me * CH_DEV, CH_DEV)], place(chunk, me), own_sem
        ).start()
        pltpu.make_async_remote_copy(
            src_ref=send.at[chunk, pl.ds(me * CH_DEV, CH_DEV)],
            dst_ref=place(chunk, me),
            send_sem=fwd_send,
            recv_sem=fwd_recv,
            device_id={"narrow": 1 - core},
            device_id_type=MESH,
        ).start()

    @pl.loop(0, chunks)
    def _(chunk):
        for d in range(1, wide):
            source = lax.rem(me + wide - d, wide)
            here = place(chunk, source)
            pltpu.make_async_copy(here, here, recv_sem.at[chunk, source]).wait()
            pltpu.make_async_remote_copy(
                src_ref=here,
                dst_ref=here,
                send_sem=fwd_send,
                recv_sem=fwd_recv,
                device_id={"narrow": 1 - core},
                device_id_type=MESH,
            ).start()

    half_out = out.at[:, :, pl.ds(0, wide * nq)]
    pltpu.make_async_copy(half_out, half_out, fwd_send).wait()
    pltpu.make_async_copy(half_out, half_out, fwd_recv).wait()
    sent = send.at[:, pl.ds(0, (wide - 1) * CH_DEV)]
    pltpu.make_async_copy(sent, sent, send_sem).wait()
    own = send.at[:, pl.ds(0, CH_DEV)]
    pltpu.make_async_copy(own, own, own_sem).wait()


def correlate(halves, order, spectra, out, pick):
    inputs = pick.shape[0]
    local = inputs // 2
    core = lax.axis_index("narrow")

    @pl.when(pl.program_id(0) == 0)
    def _():
        stations = inputs // 2
        spread = (
            lax.broadcasted_iota(jnp.int32, (stations, inputs), 0)
            == lax.broadcasted_iota(jnp.int32, (stations, inputs), 1) // 2
        ).astype(jnp.float32).astype(jnp.bfloat16)
        row = jnp.broadcast_to(order[...].astype(jnp.float32), (16, stations)).astype(jnp.bfloat16)
        wide_row = jnp.dot(row, spread, preferred_element_type=jnp.float32)[0:1]
        odd = lax.broadcasted_iota(jnp.int32, (1, inputs), 1) % 2
        column = 2 * wide_row.astype(jnp.int32) + odd
        hit = lax.broadcasted_iota(jnp.int32, (inputs, inputs), 0) == column
        pick[...] = hit.astype(jnp.float32).T.astype(jnp.bfloat16)

    lane = lax.broadcasted_iota(jnp.int32, (inputs, 2 * HALF), 1)
    sign = jnp.where(lane < HALF, -1.0, 1.0)
    rows, cols, turned = [], [], []
    for th in range(halves):
        block = spectra[th, 0]
        if block.shape[1] % 16:
            block = block.astype(jnp.float32).reshape(inputs, 2 * HALF).astype(jnp.bfloat16)
        else:
            block = block.reshape(inputs, 2 * HALF)
        rows.append(jnp.where(core == 0, block[:local], block[local:]))
        picked = jnp.dot(pick[...], block, preferred_element_type=jnp.float32)
        cols.append(picked.astype(jnp.bfloat16))
        turned.append((pltpu.roll(picked, HALF, 1) * sign).astype(jnp.bfloat16))
    left = jnp.concatenate(rows, 1)
    contract = (((1,), (1,)), ((), ()))
    for part, right in enumerate((cols, turned)):
        tile = lax.dot_general(
            left, jnp.concatenate(right, 1), contract, preferred_element_type=jnp.float32
        )
        out[0, part] = (tile * (1.0 / (halves * HALF))).astype(jnp.bfloat16)


def body(voltages, fir_taps, flags, tile_order):
    local_inputs, samples = voltages.shape[1:]
    wide = lax.axis_size("wide")
    narrow = lax.axis_size("narrow")
    times = samples // NFFT - TAPS + 1
    halves = times // HALF
    rows = 16 if local_inputs % 16 == 0 else local_inputs
    nq = local_inputs // rows
    chunks = nq * halves
    kept = CH_DEV * wide
    span = 2 * kept
    steps = HALF + TAPS - 1
    groups = narrow * wide * nq
    inputs = groups * rows
    vmem = pl.BlockSpec(memory_space=pltpu.VMEM)
    hbm = pl.BlockSpec(memory_space=pl.ANY)
    spectra = pl.pallas_call(
        functools.partial(channelise, wide, nq, rows, halves),
        out_shape=jax.ShapeDtypeStruct((halves, CH_DEV, groups, rows, 2 * HALF), jnp.bfloat16),
        in_specs=[hbm, vmem, vmem, pl.BlockSpec(memory_space=pltpu.SMEM)],
        out_specs=hbm,
        scratch_shapes=[
            pltpu.VMEM((chunks, steps, rows, 2 * NFFT), jnp.bfloat16),
            pltpu.VMEM((2 * NFFT, TAPS * span), jnp.bfloat16),
            pltpu.VMEM((steps * rows, TAPS * span), jnp.float32),
            pltpu.VMEM((span // 128, HALF * rows, 128), jnp.float32),
            pltpu.VMEM((kept * rows, 2 * HALF), jnp.float32),
            pltpu.VMEM((chunks, kept, rows, 2 * HALF), jnp.bfloat16),
            pltpu.SemaphoreType.DMA((chunks,)),
            pltpu.SemaphoreType.DMA,
            pltpu.SemaphoreType.DMA((chunks, wide)),
            pltpu.SemaphoreType.DMA,
            pltpu.SemaphoreType.DMA,
            pltpu.SemaphoreType.DMA,
        ],
        compiler_params=pltpu.CompilerParams(
            collective_id=0, has_side_effects=True, vmem_limit_bytes=60 * 1024 * 1024
        ),
        cost_estimate=pl.CostEstimate(
            flops=2 * chunks * steps * rows * 2 * NFFT * TAPS * span,
            bytes_accessed=voltages.size * 2,
            transcendentals=0,
        ),
        name="channelise",
    )(voltages, jnp.asarray(dft_table(NFFT, kept)), fir_taps, flags)
    return pl.pallas_call(
        functools.partial(correlate, halves),
        grid=(CH_DEV,),
        out_shape=jax.ShapeDtypeStruct((CH_DEV, 2, inputs // narrow, inputs), jnp.bfloat16),
        in_specs=[
            pl.BlockSpec((1, tile_order.shape[0]), lambda c: (0, 0)),
            pl.BlockSpec((halves, 1, groups, rows, 2 * HALF), lambda c: (0, c, 0, 0, 0)),
        ],
        out_specs=pl.BlockSpec((1, 2, inputs // narrow, inputs), lambda c: (c, 0, 0, 0)),
        scratch_shapes=[pltpu.VMEM((inputs, inputs), jnp.bfloat16)],
        compiler_params=pltpu.CompilerParams(vmem_limit_bytes=32 * 1024 * 1024),
        cost_estimate=pl.CostEstimate(
            flops=4 * CH_DEV * inputs * inputs * 2 * HALF * halves,
            bytes_accessed=3 * CH_DEV * inputs * inputs,
            transcendentals=0,
        ),
        name="correlate",
    )(tile_order.reshape(1, -1), spectra)


def solution(mesh):
    placed = (P(None, ("band", "narrow", "wide"), None), P(), P(("band", "narrow", "wide")), P())
    return jax.shard_map(
        body,
        mesh=mesh,
        in_specs=placed,
        out_specs=P(("band", "wide"), None, "narrow", None),
        check_vma=False,
    )
```

```python
import functools
import math

import jax
import jax.numpy as jnp
import ml_dtypes
import numpy as np
from jax import lax
from jax.experimental import pallas as pl
from jax.experimental.pallas import tpu as pltpu
from jax.sharding import PartitionSpec as P

NFFT = 2048
TAPS = 4
CH_DEV = 8
HALF = 64
MESH = pl.DeviceIdType.MESH


def dft_table(points, kept):
    phase = np.arange(points)[:, None] * np.arange(kept)[None, :] % points
    theta = phase * (2.0 * math.pi / points)
    cosine, sine = np.cos(theta), np.sin(theta)
    halves = []
    for h in range(2):
        mine = slice(h * kept // 2, (h + 1) * kept // 2)
        c, s = cosine[:, mine], sine[:, mine]
        both = np.concatenate([np.concatenate([c, -s], 1), np.concatenate([s, c], 1)], 0)
        halves.append(np.concatenate([both] * max(1, 128 // kept), 1))
    return np.stack(halves).astype(ml_dtypes.bfloat16)


def one_hot(order, inputs):
    stations = inputs // 2
    spread = (
        lax.broadcasted_iota(jnp.int32, (stations, inputs), 0)
        == lax.broadcasted_iota(jnp.int32, (stations, inputs), 1) // 2
    ).astype(jnp.float32).astype(jnp.bfloat16)
    row = jnp.broadcast_to(order.astype(jnp.float32), (16, stations)).astype(jnp.bfloat16)
    wide_row = jnp.dot(row, spread, preferred_element_type=jnp.float32)[0:1]
    odd = lax.broadcasted_iota(jnp.int32, (1, inputs), 1) % 2
    column = 2 * wide_row.astype(jnp.int32) + odd
    hit = lax.broadcasted_iota(jnp.int32, (inputs, inputs), 0) == column
    return hit.astype(jnp.float32).T.astype(jnp.bfloat16)


def channelise(wide, nq, rows, halves, volt, dft, fir, flags, order, out, pick, frames, weights,
               table, grid_sum, spec, stage, send, in_sem, dft_sem, send_sem, recv_sem, own_sem,
               fwd_send, fwd_recv):
    me = lax.axis_index("wide")
    core = lax.axis_index("narrow")
    side = me // (wide // 2)
    group = wide // 2
    kept = CH_DEV * wide
    half = kept // 2
    steps = HALF + TAPS - 1
    chunks = nq * halves
    lanes = weights.shape[1]
    fold = lanes // kept

    def weights_copy(turn):
        which = 1 - side if turn == 0 else side
        return pltpu.make_async_copy(dft.at[which], weights, dft_sem.at[turn])

    barrier = pltpu.get_barrier_semaphore()
    for d in range(1, wide):
        pl.semaphore_signal(barrier, inc=1, device_id={"wide": lax.rem(me + d, wide)}, device_id_type=MESH)
    pl.semaphore_signal(barrier, inc=1, device_id={"narrow": 1 - core}, device_id_type=MESH)

    weights_copy(0).start()

    def load(chunk):
        q, th = chunk // halves, chunk % halves

        @pl.loop(0, steps)
        def _(s):
            for part in range(2):
                pltpu.make_async_copy(
                    volt.at[part, pl.ds(q * rows, rows), pl.ds(pl.multiple_of((th * HALF + s) * NFFT, NFFT), NFFT)],
                    frames.at[chunk, s, :, pl.ds(part * NFFT, NFFT)],
                    in_sem.at[chunk],
                ).start()

    for chunk in range(chunks):
        load(chunk)

    def build():
        taps = jnp.concatenate([fir[...], fir[...]], 0).T
        step_n = 256
        lane = lax.broadcasted_iota(jnp.int32, (step_n, lanes), 1)
        for n0 in range(0, NFFT, step_n):
            scales = []
            for k in range(0, TAPS, fold):
                scale = jnp.broadcast_to(taps[n0 : n0 + step_n, k : k + 1], (step_n, lanes))
                for f in range(1, fold):
                    scale = jnp.where(lane < f * kept, scale, taps[n0 : n0 + step_n, k + f : k + f + 1])
                scales.append(scale)
            for part in range(2):
                base = part * NFFT + n0
                w = weights[base : base + step_n, :].astype(jnp.float32)
                for b, scale in enumerate(scales):
                    table[base : base + step_n, b * lanes : (b + 1) * lanes] = (w * scale).astype(jnp.bfloat16)

    def place(chunk, source):
        q, th = chunk // halves, chunk % halves
        return out.at[th, :, (core * wide + source) * nq + q]

    def to_peer(turn, chunk, peer):
        return pltpu.make_async_remote_copy(
            src_ref=send.at[turn, chunk, pl.ds(lax.rem(peer, group) * CH_DEV, CH_DEV)],
            dst_ref=place(chunk, me),
            send_sem=send_sem.at[turn],
            recv_sem=recv_sem.at[chunk, me],
            device_id={"wide": peer},
            device_id_type=MESH,
        )

    def work(turn, chunk):
        lhs = frames[chunk]
        if rows % 16:
            lhs = lhs.astype(jnp.float32).reshape(steps * rows, 2 * NFFT).astype(jnp.bfloat16)
        else:
            lhs = lhs.reshape(steps * rows, 2 * NFFT)
        grid_sum[...] = jnp.dot(lhs, table[...], preferred_element_type=jnp.float32)
        count = HALF * rows

        def tap(b, extra):
            first = b * fold * rows
            return grid_sum[first : first + count + extra * rows, b * lanes : (b + 1) * lanes]

        extra = fold - 1
        total = tap(0, extra)
        for b in range(1, TAPS // fold):
            total = total + tap(b, extra)
        if fold == 2:
            total = total[:count] + pltpu.roll(total[rows:], kept, 1)
        for b in range(lanes // 128):
            spec[b] = total[:, b * 128 : (b + 1) * 128]
        q = chunk // halves
        for i in range(rows):
            pieces = [spec[b, pl.ds(i, HALF, stride=rows), :] for b in range(lanes // 128)]
            if half % 128:
                piece = pieces[0]
                both = jnp.concatenate([piece, pltpu.roll(piece, 128 - half, 1)], 0).T[:half]
            else:
                mid = half // 128
                both = jnp.concatenate(
                    [jnp.concatenate([pieces[b], pieces[mid + b]], 0).T for b in range(mid)], 0
                )
            both = both * flags[q * rows + i].astype(jnp.float32)
            stage[pl.ds(i, half, stride=rows), :] = both
        send[turn, chunk] = stage[...].reshape(half, rows, 2 * HALF).astype(jnp.bfloat16)

    weights_copy(0).wait()
    build()
    weights_copy(1).start()
    pl.semaphore_wait(barrier, wide)

    @pl.loop(0, chunks)
    def _(chunk):
        pltpu.make_async_copy(frames.at[chunk], frames.at[chunk], in_sem.at[chunk]).wait()
        work(0, chunk)
        for d in range(group, wide):
            to_peer(0, chunk, me ^ d).start()

    weights_copy(1).wait()
    build()

    @pl.loop(0, chunks)
    def _(chunk):
        work(1, chunk)
        for d in range(1, group):
            to_peer(1, chunk, me ^ d).start()
        own = send.at[1, chunk, pl.ds(lax.rem(me, group) * CH_DEV, CH_DEV)]
        pltpu.make_async_copy(own, place(chunk, me), own_sem).start()
        pltpu.make_async_remote_copy(
            src_ref=own,
            dst_ref=place(chunk, me),
            send_sem=fwd_send,
            recv_sem=fwd_recv,
            device_id={"narrow": 1 - core},
            device_id_type=MESH,
        ).start()

    pick[...] = one_hot(order[...], pick.shape[0])

    def forward(chunk, d):
        source = me ^ d
        here = place(chunk, source)
        pltpu.make_async_copy(here, here, recv_sem.at[chunk, source]).wait()
        pltpu.make_async_remote_copy(
            src_ref=here,
            dst_ref=here,
            send_sem=fwd_send,
            recv_sem=fwd_recv,
            device_id={"narrow": 1 - core},
            device_id_type=MESH,
        ).start()

    def forward_all(low, high, first, last):
        @pl.loop(first, last)
        def _(chunk):
            for d in range(low, high):
                forward(chunk, d)

    forward_all(group, wide, 0, chunks - 1)
    forward_all(1, group, 0, chunks)
    forward_all(group, wide, chunks - 1, chunks)

    half_out = out.at[:, :, pl.ds(0, wide * nq)]
    pltpu.make_async_copy(half_out, half_out, fwd_send).wait()
    pltpu.make_async_copy(half_out, half_out, fwd_recv).wait()
    pltpu.make_async_copy(send.at[0], send.at[0], send_sem.at[0]).wait()
    if group > 1:
        sent = send.at[1, :, pl.ds(0, (group - 1) * CH_DEV)]
        pltpu.make_async_copy(sent, sent, send_sem.at[1]).wait()
    own = send.at[1, :, pl.ds(0, CH_DEV)]
    pltpu.make_async_copy(own, own, own_sem).wait()


def flat(block):
    count = block.shape[0] * block.shape[1]
    if block.shape[1] % 16:
        return block.astype(jnp.float32).reshape(count, 2 * HALF).astype(jnp.bfloat16)
    return block.reshape(count, 2 * HALF)


def correlate(halves, pick, spectra, out):
    inputs = pick.shape[0]
    mine = spectra.shape[2] // 2
    core = lax.axis_index("narrow")
    lane = lax.broadcasted_iota(jnp.int32, (inputs, 2 * HALF), 1)
    sign = jnp.where(lane < HALF, -1.0, 1.0)
    rows, cols, turned = [], [], []
    for th in range(halves):
        block = flat(spectra[th, 0])
        rows.append(flat(spectra[th, 0, pl.ds(core * mine, mine)]))
        picked = jnp.dot(pick[...], block, preferred_element_type=jnp.float32)
        cols.append(picked.astype(jnp.bfloat16))
        turned.append((pltpu.roll(picked, HALF, 1) * sign).astype(jnp.bfloat16))
    left = jnp.concatenate(rows, 1)
    contract = (((1,), (1,)), ((), ()))
    for part, right in enumerate((cols, turned)):
        tile = lax.dot_general(
            left, jnp.concatenate(right, 1), contract, preferred_element_type=jnp.float32
        )
        out[0, part] = (tile * (1.0 / (halves * HALF))).astype(jnp.bfloat16)


def body(voltages, fir_taps, flags, tile_order):
    local_inputs, samples = voltages.shape[1:]
    wide = lax.axis_size("wide")
    narrow = lax.axis_size("narrow")
    times = samples // NFFT - TAPS + 1
    halves = times // HALF
    rows = 16 if local_inputs % 16 == 0 else local_inputs
    nq = local_inputs // rows
    chunks = nq * halves
    kept = CH_DEV * wide
    steps = HALF + TAPS - 1
    groups = narrow * wide * nq
    inputs = groups * rows
    lanes = max(kept, 128)
    vmem = pl.BlockSpec(memory_space=pltpu.VMEM)
    hbm = pl.BlockSpec(memory_space=pl.ANY)
    spectra, pick = pl.pallas_call(
        functools.partial(channelise, wide, nq, rows, halves),
        out_shape=(
            jax.ShapeDtypeStruct((halves, CH_DEV, groups, rows, 2 * HALF), jnp.bfloat16),
            jax.ShapeDtypeStruct((inputs, inputs), jnp.bfloat16),
        ),
        in_specs=[hbm, hbm, vmem, pl.BlockSpec(memory_space=pltpu.SMEM), vmem],
        out_specs=(hbm, vmem),
        scratch_shapes=[
            pltpu.VMEM((chunks, steps, rows, 2 * NFFT), jnp.bfloat16),
            pltpu.VMEM((2 * NFFT, lanes), jnp.bfloat16),
            pltpu.VMEM((2 * NFFT, TAPS * kept), jnp.bfloat16),
            pltpu.VMEM((steps * rows, TAPS * kept), jnp.float32),
            pltpu.VMEM((lanes // 128, HALF * rows, 128), jnp.float32),
            pltpu.VMEM((kept // 2 * rows, 2 * HALF), jnp.float32),
            pltpu.VMEM((2, chunks, kept // 2, rows, 2 * HALF), jnp.bfloat16),
            pltpu.SemaphoreType.DMA((chunks,)),
            pltpu.SemaphoreType.DMA((2,)),
            pltpu.SemaphoreType.DMA((2,)),
            pltpu.SemaphoreType.DMA((chunks, wide)),
            pltpu.SemaphoreType.DMA,
            pltpu.SemaphoreType.DMA,
            pltpu.SemaphoreType.DMA,
        ],
        compiler_params=pltpu.CompilerParams(
            collective_id=0, has_side_effects=True, vmem_limit_bytes=60 * 1024 * 1024
        ),
        cost_estimate=pl.CostEstimate(
            flops=4 * chunks * steps * rows * 2 * NFFT * TAPS * kept,
            bytes_accessed=voltages.size * 2,
            transcendentals=0,
        ),
        name="channelise",
    )(voltages, jnp.asarray(dft_table(NFFT, kept)), fir_taps, flags, tile_order.reshape(1, -1))
    return pl.pallas_call(
        functools.partial(correlate, halves),
        grid=(CH_DEV,),
        out_shape=jax.ShapeDtypeStruct((CH_DEV, 2, inputs // narrow, inputs), jnp.bfloat16),
        in_specs=[
            pl.BlockSpec((inputs, inputs), lambda c: (0, 0)),
            pl.BlockSpec((halves, 1, groups, rows, 2 * HALF), lambda c: (0, c, 0, 0, 0)),
        ],
        out_specs=pl.BlockSpec((1, 2, inputs // narrow, inputs), lambda c: (c, 0, 0, 0)),
        compiler_params=pltpu.CompilerParams(vmem_limit_bytes=32 * 1024 * 1024),
        cost_estimate=pl.CostEstimate(
            flops=4 * CH_DEV * inputs * inputs * 2 * HALF * halves,
            bytes_accessed=3 * CH_DEV * inputs * inputs,
            transcendentals=0,
        ),
        name="correlate",
    )(pick, spectra)


def solution(mesh):
    placed = (P(None, ("band", "narrow", "wide"), None), P(), P(("band", "narrow", "wide")), P())
    return jax.shard_map(
        body,
        mesh=mesh,
        in_specs=placed,
        out_specs=P(("band", "wide"), None, "narrow", None),
        check_vma=False,
    )
```

```python
import functools
import math

import jax
import jax.numpy as jnp
import ml_dtypes
import numpy as np
from jax import lax
from jax.experimental import pallas as pl
from jax.experimental.pallas import tpu as pltpu
from jax.sharding import PartitionSpec as P

NFFT = 2048
TAPS = 4
CH_DEV = 8
CH_STEP = 4
HALF = 64
MESH = pl.DeviceIdType.MESH


def dft_table(points, kept):
    phase = np.arange(points)[:, None] * np.arange(kept)[None, :] % points
    theta = phase * (2.0 * math.pi / points)
    cosine, sine = np.cos(theta), np.sin(theta)
    upper = np.concatenate([cosine, -sine], 1)
    lower = np.concatenate([sine, cosine], 1)
    return np.concatenate([upper, lower], 0).astype(ml_dtypes.bfloat16)


def one_hot(order, inputs):
    stations = inputs // 2
    spread = (
        lax.broadcasted_iota(jnp.int32, (stations, inputs), 0)
        == lax.broadcasted_iota(jnp.int32, (stations, inputs), 1) // 2
    ).astype(jnp.float32).astype(jnp.bfloat16)
    row = jnp.broadcast_to(order.astype(jnp.float32), (16, stations)).astype(jnp.bfloat16)
    wide_row = jnp.dot(row, spread, preferred_element_type=jnp.float32)[0:1]
    odd = lax.broadcasted_iota(jnp.int32, (1, inputs), 1) % 2
    column = 2 * wide_row.astype(jnp.int32) + odd
    hit = lax.broadcasted_iota(jnp.int32, (inputs, inputs), 0) == column
    return hit.astype(jnp.float32).T.astype(jnp.bfloat16)


def channelise(wide, nq, rows, halves, volt, dft, fir, flags, order, out, pick, frames, table, grid_sum, spec,
               stage, send, in_sem, send_sem, recv_sem, own_sem, fwd_send, fwd_recv):
    me = lax.axis_index("wide")
    core = lax.axis_index("narrow")
    kept = CH_DEV * wide
    span = 2 * kept
    steps = HALF + TAPS - 1
    chunks = nq * halves

    def load(chunk):
        q, th = chunk // halves, chunk % halves

        for s in range(steps):
            for part in range(2):
                pltpu.make_async_copy(
                    volt.at[part, pl.ds(q * rows, rows), pl.ds(pl.multiple_of((th * HALF + s) * NFFT, NFFT), NFFT)],
                    frames.at[chunk, s, :, pl.ds(part * NFFT, NFFT)],
                    in_sem.at[chunk],
                ).start()

    barrier = pltpu.get_barrier_semaphore()
    for d in range(1, wide):
        pl.semaphore_signal(barrier, inc=1, device_id={"wide": lax.rem(me + d, wide)}, device_id_type=MESH)
    pl.semaphore_signal(barrier, inc=1, device_id={"narrow": 1 - core}, device_id_type=MESH)

    load(0)
    taps = jnp.concatenate([fir[...], fir[...]], 0).T
    step_n = 256
    for n0 in range(0, NFFT, step_n):
        for part in range(2):
            base = part * NFFT + n0
            w = dft[base : base + step_n, :].astype(jnp.float32)
            for k in range(TAPS):
                table[base : base + step_n, k * span : (k + 1) * span] = (
                    w * taps[n0 : n0 + step_n, k : k + 1]
                ).astype(jnp.bfloat16)

    pl.semaphore_wait(barrier, wide)

    def place(chunk, source):
        q, th = chunk // halves, chunk % halves
        return out.at[th, :, (core * wide + source) * nq + q]

    def to_peer(chunk, peer):
        return pltpu.make_async_remote_copy(
            src_ref=send.at[chunk, pl.ds(peer * CH_DEV, CH_DEV)],
            dst_ref=place(chunk, me),
            send_sem=send_sem,
            recv_sem=recv_sem.at[chunk, me],
            device_id={"wide": peer},
            device_id_type=MESH,
        )

    @pl.loop(0, chunks)
    def _(chunk):
        @pl.when(chunk + 1 < chunks)
        def _():
            load(chunk + 1)

        pltpu.make_async_copy(frames.at[chunk], frames.at[chunk], in_sem.at[chunk]).wait()
        lhs = frames[chunk]
        if rows % 16:
            lhs = lhs.astype(jnp.float32).reshape(steps * rows, 2 * NFFT).astype(jnp.bfloat16)
        else:
            lhs = lhs.reshape(steps * rows, 2 * NFFT)
        grid_sum[...] = jnp.dot(lhs, table[...], preferred_element_type=jnp.float32)
        count = HALF * rows
        total = grid_sum[0:count, 0:span]
        for k in range(1, TAPS):
            total = total + grid_sum[k * rows : k * rows + count, k * span : (k + 1) * span]
        for lane in range(0, span, 128):
            spec[lane // 128] = total[:, lane : lane + 128]
        q = chunk // halves
        for i in range(rows):
            pieces = [spec[b, pl.ds(i, HALF, stride=rows), :] for b in range(span // 128)]
            if kept % 128:
                piece = pieces[0]
                both = jnp.concatenate([piece, pltpu.roll(piece, kept, 1)], 0).T[:kept]
            else:
                mid = kept // 128
                both = jnp.concatenate(
                    [jnp.concatenate([pieces[b], pieces[mid + b]], 0).T for b in range(mid)], 0
                )
            both = both * flags[q * rows + i].astype(jnp.float32)
            stage[pl.ds(i, kept, stride=rows), :] = both
        send[chunk] = stage[...].reshape(kept, rows, 2 * HALF).astype(jnp.bfloat16)
        for d in range(1, wide):
            to_peer(chunk, lax.rem(me + d, wide)).start()
        pltpu.make_async_copy(
            send.at[chunk, pl.ds(me * CH_DEV, CH_DEV)], place(chunk, me), own_sem
        ).start()
        pltpu.make_async_remote_copy(
            src_ref=send.at[chunk, pl.ds(me * CH_DEV, CH_DEV)],
            dst_ref=place(chunk, me),
            send_sem=fwd_send,
            recv_sem=fwd_recv,
            device_id={"narrow": 1 - core},
            device_id_type=MESH,
        ).start()

    pick[...] = one_hot(order[...], pick.shape[0])

    @pl.loop(0, chunks)
    def _(chunk):
        for d in range(1, wide):
            source = lax.rem(me + wide - d, wide)
            here = place(chunk, source)
            pltpu.make_async_copy(here, here, recv_sem.at[chunk, source]).wait()
            pltpu.make_async_remote_copy(
                src_ref=here,
                dst_ref=here,
                send_sem=fwd_send,
                recv_sem=fwd_recv,
                device_id={"narrow": 1 - core},
                device_id_type=MESH,
            ).start()

    half_out = out.at[:, :, pl.ds(0, wide * nq)]
    pltpu.make_async_copy(half_out, half_out, fwd_send).wait()
    pltpu.make_async_copy(half_out, half_out, fwd_recv).wait()
    sent = send.at[:, pl.ds(0, (wide - 1) * CH_DEV)]
    pltpu.make_async_copy(sent, sent, send_sem).wait()
    own = send.at[:, pl.ds(0, CH_DEV)]
    pltpu.make_async_copy(own, own, own_sem).wait()


def flat(block):
    count = block.shape[0] * block.shape[1]
    if block.shape[1] % 16:
        return block.astype(jnp.float32).reshape(count, 2 * HALF).astype(jnp.bfloat16)
    return block.reshape(count, 2 * HALF)


def correlate(halves, pick, spectra, out):
    mine = spectra.shape[2] // 2
    core = lax.axis_index("narrow")
    contract = (((1,), (1,)), ((), ()))
    for c in range(out.shape[0]):
        block = jnp.concatenate([flat(spectra[th, c]) for th in range(halves)], 1)
        left = jnp.concatenate(
            [flat(spectra[th, c, pl.ds(core * mine, mine)]) for th in range(halves)], 1
        )
        picked = jnp.dot(pick[...], block, preferred_element_type=jnp.float32)
        lane = lax.broadcasted_iota(jnp.int32, (picked.shape[0], 2 * HALF), 1)
        sign = jnp.where(lane < HALF, -1.0, 1.0)
        turned = jnp.concatenate(
            [pltpu.roll(picked[:, b * 128 : (b + 1) * 128], HALF, 1) * sign for b in range(halves)], 1
        )
        for part, right in enumerate((picked, turned)):
            tile = lax.dot_general(
                left, right.astype(jnp.bfloat16), contract, preferred_element_type=jnp.float32
            )
            out[c, part] = (tile * (1.0 / (halves * HALF))).astype(jnp.bfloat16)


def body(voltages, fir_taps, flags, tile_order):
    local_inputs, samples = voltages.shape[1:]
    wide = lax.axis_size("wide")
    narrow = lax.axis_size("narrow")
    times = samples // NFFT - TAPS + 1
    halves = times // HALF
    rows = 16 if local_inputs % 16 == 0 else local_inputs
    nq = local_inputs // rows
    chunks = nq * halves
    kept = CH_DEV * wide
    span = 2 * kept
    steps = HALF + TAPS - 1
    groups = narrow * wide * nq
    inputs = groups * rows
    vmem = pl.BlockSpec(memory_space=pltpu.VMEM)
    hbm = pl.BlockSpec(memory_space=pl.ANY)
    spectra, pick = pl.pallas_call(
        functools.partial(channelise, wide, nq, rows, halves),
        out_shape=(
            jax.ShapeDtypeStruct((halves, CH_DEV, groups, rows, 2 * HALF), jnp.bfloat16),
            jax.ShapeDtypeStruct((inputs, inputs), jnp.bfloat16),
        ),
        in_specs=[hbm, vmem, vmem, pl.BlockSpec(memory_space=pltpu.SMEM), vmem],
        out_specs=(hbm, vmem),
        scratch_shapes=[
            pltpu.VMEM((chunks, steps, rows, 2 * NFFT), jnp.bfloat16),
            pltpu.VMEM((2 * NFFT, TAPS * span), jnp.bfloat16),
            pltpu.VMEM((steps * rows, TAPS * span), jnp.float32),
            pltpu.VMEM((span // 128, HALF * rows, 128), jnp.float32),
            pltpu.VMEM((kept * rows, 2 * HALF), jnp.float32),
            pltpu.VMEM((chunks, kept, rows, 2 * HALF), jnp.bfloat16),
            pltpu.SemaphoreType.DMA((chunks,)),
            pltpu.SemaphoreType.DMA,
            pltpu.SemaphoreType.DMA((chunks, wide)),
            pltpu.SemaphoreType.DMA,
            pltpu.SemaphoreType.DMA,
            pltpu.SemaphoreType.DMA,
        ],
        compiler_params=pltpu.CompilerParams(
            collective_id=0, has_side_effects=True, vmem_limit_bytes=60 * 1024 * 1024
        ),
        cost_estimate=pl.CostEstimate(
            flops=2 * chunks * steps * rows * 2 * NFFT * TAPS * span,
            bytes_accessed=voltages.size * 2,
            transcendentals=0,
        ),
        name="channelise",
    )(voltages, jnp.asarray(dft_table(NFFT, kept)), fir_taps, flags, tile_order.reshape(1, -1))
    return pl.pallas_call(
        functools.partial(correlate, halves),
        grid=(CH_DEV // CH_STEP,),
        out_shape=jax.ShapeDtypeStruct((CH_DEV, 2, inputs // narrow, inputs), jnp.bfloat16),
        in_specs=[
            pl.BlockSpec((inputs, inputs), lambda c: (0, 0)),
            pl.BlockSpec((halves, CH_STEP, groups, rows, 2 * HALF), lambda c: (0, c, 0, 0, 0)),
        ],
        out_specs=pl.BlockSpec((CH_STEP, 2, inputs // narrow, inputs), lambda c: (c, 0, 0, 0)),
        compiler_params=pltpu.CompilerParams(vmem_limit_bytes=60 * 1024 * 1024),
        cost_estimate=pl.CostEstimate(
            flops=4 * CH_DEV * inputs * inputs * 2 * HALF * halves,
            bytes_accessed=3 * CH_DEV * inputs * inputs,
            transcendentals=0,
        ),
        name="correlate",
    )(pick, spectra)


def solution(mesh):
    placed = (P(None, ("band", "narrow", "wide"), None), P(), P(("band", "narrow", "wide")), P())
    return jax.shard_map(
        body,
        mesh=mesh,
        in_specs=placed,
        out_specs=P(("band", "wide"), None, "narrow", None),
        check_vma=False,
    )
```

```python
import functools
import math

import jax
import jax.numpy as jnp
import ml_dtypes
import numpy as np
from jax import lax
from jax.experimental import pallas as pl
from jax.experimental.pallas import tpu as pltpu
from jax.sharding import PartitionSpec as P

NFFT = 2048
TAPS = 4
CH_DEV = 8
CH_STEP = 4
SPLIT = [0, 34]
HALF = 64
MESH = pl.DeviceIdType.MESH


def dft_table(points, kept):
    phase = np.arange(points)[:, None] * np.arange(kept)[None, :] % points
    theta = phase * (2.0 * math.pi / points)
    cosine, sine = np.cos(theta), np.sin(theta)
    upper = np.concatenate([cosine, -sine], 1)
    lower = np.concatenate([sine, cosine], 1)
    return np.concatenate([upper, lower], 0).astype(ml_dtypes.bfloat16)


def one_hot(order, inputs):
    stations = inputs // 2
    spread = (
        lax.broadcasted_iota(jnp.int32, (stations, inputs), 0)
        == lax.broadcasted_iota(jnp.int32, (stations, inputs), 1) // 2
    ).astype(jnp.float32).astype(jnp.bfloat16)
    row = jnp.broadcast_to(order.astype(jnp.float32), (16, stations)).astype(jnp.bfloat16)
    wide_row = jnp.dot(row, spread, preferred_element_type=jnp.float32)[0:1]
    odd = lax.broadcasted_iota(jnp.int32, (1, inputs), 1) % 2
    column = 2 * wide_row.astype(jnp.int32) + odd
    hit = lax.broadcasted_iota(jnp.int32, (inputs, inputs), 0) == column
    return hit.astype(jnp.float32).T.astype(jnp.bfloat16)


def channelise(wide, nq, rows, halves, volt, dft, fir, flags, order, out, pick, frames, table, grid_sum, spec,
               stage, send, in_sem, send_sem, recv_sem, own_sem, fwd_send, fwd_recv):
    me = lax.axis_index("wide")
    core = lax.axis_index("narrow")
    kept = CH_DEV * wide
    span = 2 * kept
    steps = HALF + TAPS - 1
    chunks = nq * halves
    split = SPLIT

    def load(chunk):
        q, th = chunk // halves, chunk % halves

        for s in range(steps):
            for part in range(2):
                pltpu.make_async_copy(
                    volt.at[part, pl.ds(q * rows, rows), pl.ds(pl.multiple_of((th * HALF + s) * NFFT, NFFT), NFFT)],
                    frames.at[chunk, s, :, pl.ds(part * NFFT, NFFT)],
                    in_sem.at[chunk, split.index(max(x for x in split if x <= s))],
                ).start()

    barrier = pltpu.get_barrier_semaphore()
    for d in range(1, wide):
        pl.semaphore_signal(barrier, inc=1, device_id={"wide": lax.rem(me + d, wide)}, device_id_type=MESH)
    pl.semaphore_signal(barrier, inc=1, device_id={"narrow": 1 - core}, device_id_type=MESH)

    load(0)
    taps = jnp.concatenate([fir[...], fir[...]], 0).T
    step_n = 256
    for n0 in range(0, NFFT, step_n):
        for part in range(2):
            base = part * NFFT + n0
            w = dft[base : base + step_n, :].astype(jnp.float32)
            for k in range(TAPS):
                table[base : base + step_n, k * span : (k + 1) * span] = (
                    w * taps[n0 : n0 + step_n, k : k + 1]
                ).astype(jnp.bfloat16)

    pl.semaphore_wait(barrier, wide)

    def place(chunk, source):
        q, th = chunk // halves, chunk % halves
        return out.at[th, :, (core * wide + source) * nq + q]

    def to_peer(chunk, peer):
        return pltpu.make_async_remote_copy(
            src_ref=send.at[chunk, pl.ds(peer * CH_DEV, CH_DEV)],
            dst_ref=place(chunk, me),
            send_sem=send_sem,
            recv_sem=recv_sem.at[chunk, me],
            device_id={"wide": peer},
            device_id_type=MESH,
        )

    @pl.loop(0, chunks)
    def _(chunk):
        @pl.when(chunk + 1 < chunks)
        def _():
            load(chunk + 1)

        for b, first in enumerate(split):
            last = (split + [steps])[b + 1]
            here = frames.at[chunk, pl.ds(first, last - first)]
            pltpu.make_async_copy(here, here, in_sem.at[chunk, b]).wait()
            lhs = frames[chunk, first:last]
            if rows % 16:
                lhs = lhs.astype(jnp.float32).reshape((last - first) * rows, 2 * NFFT).astype(jnp.bfloat16)
            else:
                lhs = lhs.reshape((last - first) * rows, 2 * NFFT)
            grid_sum[first * rows : last * rows] = jnp.dot(
                lhs, table[...], preferred_element_type=jnp.float32
            )
        count = HALF * rows
        total = grid_sum[0:count, 0:span]
        for k in range(1, TAPS):
            total = total + grid_sum[k * rows : k * rows + count, k * span : (k + 1) * span]
        for lane in range(0, span, 128):
            spec[lane // 128] = total[:, lane : lane + 128]
        q = chunk // halves
        for i in range(rows):
            pieces = [spec[b, pl.ds(i, HALF, stride=rows), :] for b in range(span // 128)]
            if kept % 128:
                piece = pieces[0]
                both = jnp.concatenate([piece, pltpu.roll(piece, kept, 1)], 0).T[:kept]
            else:
                mid = kept // 128
                both = jnp.concatenate(
                    [jnp.concatenate([pieces[b], pieces[mid + b]], 0).T for b in range(mid)], 0
                )
            both = both * flags[q * rows + i].astype(jnp.float32)
            stage[pl.ds(i, kept, stride=rows), :] = both
        send[chunk] = stage[...].reshape(kept, rows, 2 * HALF).astype(jnp.bfloat16)
        for d in range(1, wide):
            to_peer(chunk, lax.rem(me + d, wide)).start()
        pltpu.make_async_copy(
            send.at[chunk, pl.ds(me * CH_DEV, CH_DEV)], place(chunk, me), own_sem
        ).start()
        pltpu.make_async_remote_copy(
            src_ref=send.at[chunk, pl.ds(me * CH_DEV, CH_DEV)],
            dst_ref=place(chunk, me),
            send_sem=fwd_send,
            recv_sem=fwd_recv,
            device_id={"narrow": 1 - core},
            device_id_type=MESH,
        ).start()

    pick[...] = one_hot(order[...], pick.shape[0])

    @pl.loop(0, chunks)
    def _(chunk):
        for d in range(1, wide):
            source = lax.rem(me + wide - d, wide)
            here = place(chunk, source)
            pltpu.make_async_copy(here, here, recv_sem.at[chunk, source]).wait()
            pltpu.make_async_remote_copy(
                src_ref=here,
                dst_ref=here,
                send_sem=fwd_send,
                recv_sem=fwd_recv,
                device_id={"narrow": 1 - core},
                device_id_type=MESH,
            ).start()

    half_out = out.at[:, :, pl.ds(0, wide * nq)]
    pltpu.make_async_copy(half_out, half_out, fwd_send).wait()
    pltpu.make_async_copy(half_out, half_out, fwd_recv).wait()
    sent = send.at[:, pl.ds(0, (wide - 1) * CH_DEV)]
    pltpu.make_async_copy(sent, sent, send_sem).wait()
    own = send.at[:, pl.ds(0, CH_DEV)]
    pltpu.make_async_copy(own, own, own_sem).wait()


def flat(block):
    count = block.shape[0] * block.shape[1]
    if block.shape[1] % 16:
        return block.astype(jnp.float32).reshape(count, 2 * HALF).astype(jnp.bfloat16)
    return block.reshape(count, 2 * HALF)


def correlate(halves, pick, spectra, out):
    mine = spectra.shape[2] // 2
    core = lax.axis_index("narrow")
    contract = (((1,), (1,)), ((), ()))
    for c in range(out.shape[0]):
        block = jnp.concatenate([flat(spectra[th, c]) for th in range(halves)], 1)
        left = jnp.concatenate(
            [flat(spectra[th, c, pl.ds(core * mine, mine)]) for th in range(halves)], 1
        )
        picked = jnp.dot(pick[...], block, preferred_element_type=jnp.float32)
        lane = lax.broadcasted_iota(jnp.int32, (picked.shape[0], 2 * HALF), 1)
        sign = jnp.where(lane < HALF, -1.0, 1.0)
        turned = jnp.concatenate(
            [pltpu.roll(picked[:, b * 128 : (b + 1) * 128], HALF, 1) * sign for b in range(halves)], 1
        )
        for part, right in enumerate((picked, turned)):
            tile = lax.dot_general(
                left, right.astype(jnp.bfloat16), contract, preferred_element_type=jnp.float32
            )
            out[c, part] = (tile * (1.0 / (halves * HALF))).astype(jnp.bfloat16)


def body(voltages, fir_taps, flags, tile_order):
    local_inputs, samples = voltages.shape[1:]
    wide = lax.axis_size("wide")
    narrow = lax.axis_size("narrow")
    times = samples // NFFT - TAPS + 1
    halves = times // HALF
    rows = 16 if local_inputs % 16 == 0 else local_inputs
    nq = local_inputs // rows
    chunks = nq * halves
    kept = CH_DEV * wide
    span = 2 * kept
    steps = HALF + TAPS - 1
    groups = narrow * wide * nq
    inputs = groups * rows
    vmem = pl.BlockSpec(memory_space=pltpu.VMEM)
    hbm = pl.BlockSpec(memory_space=pl.ANY)
    spectra, pick = pl.pallas_call(
        functools.partial(channelise, wide, nq, rows, halves),
        out_shape=(
            jax.ShapeDtypeStruct((halves, CH_DEV, groups, rows, 2 * HALF), jnp.bfloat16),
            jax.ShapeDtypeStruct((inputs, inputs), jnp.bfloat16),
        ),
        in_specs=[hbm, vmem, vmem, pl.BlockSpec(memory_space=pltpu.SMEM), vmem],
        out_specs=(hbm, vmem),
        scratch_shapes=[
            pltpu.VMEM((chunks, steps, rows, 2 * NFFT), jnp.bfloat16),
            pltpu.VMEM((2 * NFFT, TAPS * span), jnp.bfloat16),
            pltpu.VMEM((steps * rows, TAPS * span), jnp.float32),
            pltpu.VMEM((span // 128, HALF * rows, 128), jnp.float32),
            pltpu.VMEM((kept * rows, 2 * HALF), jnp.float32),
            pltpu.VMEM((chunks, kept, rows, 2 * HALF), jnp.bfloat16),
            pltpu.SemaphoreType.DMA((chunks, len(SPLIT))),
            pltpu.SemaphoreType.DMA,
            pltpu.SemaphoreType.DMA((chunks, wide)),
            pltpu.SemaphoreType.DMA,
            pltpu.SemaphoreType.DMA,
            pltpu.SemaphoreType.DMA,
        ],
        compiler_params=pltpu.CompilerParams(
            collective_id=0, has_side_effects=True, vmem_limit_bytes=60 * 1024 * 1024
        ),
        cost_estimate=pl.CostEstimate(
            flops=2 * chunks * steps * rows * 2 * NFFT * TAPS * span,
            bytes_accessed=voltages.size * 2,
            transcendentals=0,
        ),
        name="channelise",
    )(voltages, jnp.asarray(dft_table(NFFT, kept)), fir_taps, flags, tile_order.reshape(1, -1))
    return pl.pallas_call(
        functools.partial(correlate, halves),
        grid=(CH_DEV // CH_STEP,),
        out_shape=jax.ShapeDtypeStruct((CH_DEV, 2, inputs // narrow, inputs), jnp.bfloat16),
        in_specs=[
            pl.BlockSpec((inputs, inputs), lambda c: (0, 0)),
            pl.BlockSpec((halves, CH_STEP, groups, rows, 2 * HALF), lambda c: (0, c, 0, 0, 0)),
        ],
        out_specs=pl.BlockSpec((CH_STEP, 2, inputs // narrow, inputs), lambda c: (c, 0, 0, 0)),
        compiler_params=pltpu.CompilerParams(vmem_limit_bytes=60 * 1024 * 1024),
        cost_estimate=pl.CostEstimate(
            flops=4 * CH_DEV * inputs * inputs * 2 * HALF * halves,
            bytes_accessed=3 * CH_DEV * inputs * inputs,
            transcendentals=0,
        ),
        name="correlate",
    )(pick, spectra)


def solution(mesh):
    placed = (P(None, ("band", "narrow", "wide"), None), P(), P(("band", "narrow", "wide")), P())
    return jax.shard_map(
        body,
        mesh=mesh,
        in_specs=placed,
        out_specs=P(("band", "wide"), None, "narrow", None),
        check_vma=False,
    )
```
